512 devices in a mesh: pool: 32 (over x, z_hi, y), tp: 16 (over z_lo, core).
Axes of the slice: x: 4, y: 4, z: 16 (z_hi: 2, z_lo: 8; z = z_hi * 8 + z_lo), core: 2. Of those that a mesh axis runs over, the one named last changes fastest.
Arguments:
- tokens: bfloat16 [6144, 8192], P('pool', 'tp'), may hold values from -6 to 6
- norm_gain: float32 [8192], replicated, may hold values from 0.1 to 1.9
- doc_lengths: int32 [32, 4], P('pool'), may hold values from 1 to 96, 192 in all within a row
- query_master: float32 [8192, 4096], P('pool', 'tp')
- query_grad: bfloat16 [8192, 4096], P('pool', 'tp'), may hold values from -12 to 12
- query_first: float32 [8192, 4096], P('pool', 'tp'), may hold values from -6 to 6
- query_second: float32 [8192, 4096], P('pool', 'tp'), may hold values from 0.1 to 4
- kv_master: float32 [2, 8192, 512], P(None, 'pool', 'tp')
- kv_grad: bfloat16 [2, 8192, 512], P(None, 'pool', 'tp'), may hold values from -12 to 12
- kv_first: float32 [2, 8192, 512], P(None, 'pool', 'tp'), may hold values from -6 to 6
- kv_second: float32 [2, 8192, 512], P(None, 'pool', 'tp'), may hold values from 0.1 to 4
- out_master: float32 [4096, 8192], P(('tp', 'pool')), may hold values from -0.09375 to 0.09375
- out_grad: bfloat16 [4096, 8192], P(('tp', 'pool')), may hold values from -12 to 12
- out_first: float32 [4096, 8192], P(('tp', 'pool')), may hold values from -6 to 6
- out_second: float32 [4096, 8192], P(('tp', 'pool')), may hold values from 0.1 to 4
Outputs:
- mixed: bfloat16 [6144, 8192], P('pool', 'tp')
- query_master_new: float32 [8192, 4096], P('pool', 'tp')
- query_first_new: float32 [8192, 4096], P('pool', 'tp')
- query_second_new: float32 [8192, 4096], P('pool', 'tp')
- kv_master_new: float32 [2, 8192, 512], P(None, 'pool', 'tp')
- kv_first_new: float32 [2, 8192, 512], P(None, 'pool', 'tp')
- kv_second_new: float32 [2, 8192, 512], P(None, 'pool', 'tp')
- out_master_new: float32 [4096, 8192], P(('tp', 'pool'))
- out_first_new: float32 [4096, 8192], P(('tp', 'pool'))
- out_second_new: float32 [4096, 8192], P(('tp', 'pool'))
The draws below stay inside these ranges and needn't reach their ends.
Inputs may be any that keep to these rules, and one draw needn't show every extreme that they name: `doc_lengths`: each row holds the lengths of the 4 rollouts of one group and sums to 192; the longest rollout of each row has exactly 96 tokens.
All inputs are finite; a program needn't handle non-finite values.
Results may differ from the reference program's by a relative error of at most 0.023.
Values may be sent and summed in bfloat16 or wider, within the bound.
No kernel may reach another device: no remote copies, remote signals or barrier semaphores. Data moves between devices by JAX's collectives and lax.ppermute only.
A program may use at most 64 MiB of HBM per device.

```python
import math
import jax
import jax.numpy as jnp
import numpy as np
from jax import lax

D = 8192
HEAD_DIM = 128
HEADS = 32
KV_HEADS = 4
TOK_DEV = 192
DOCS = 4
QW = 4096
KVW = 512
TOKENS = 6144
N_POOL = 32
N_TP = 16


def draw_query_master(key, part):
    key = jax.random.fold_in(key, 11)
    fresh = jax.random.normal(key, (D, HEADS * HEAD_DIM), jnp.float32)
    return fresh * D ** (-0.5)


def draw_kv_master(key, part):
    key = jax.random.fold_in(key, 12)
    fresh = jax.random.normal(key, (2, D, KV_HEADS * HEAD_DIM), jnp.float32)
    return fresh * D ** (-0.5)


def levels(own_key, extent, shards, smallest, largest):
    gain, own = 1.0, jax.random.fold_in(own_key, 6)
    for axis_at, parts in shards:
        steps = jnp.exp(jax.random.uniform(jax.random.fold_in(own, axis_at), (parts,), jnp.float32, smallest / len(shards), largest / len(shards)))
        gain = gain * jnp.repeat(steps, extent[axis_at] // parts).reshape([-1 if axis == axis_at else 1 for axis in range(len(extent))])
    return gain


def length_profile(count, total, limit, slope):
    loads = [(1 << 20) // math.isqrt(grade ** slope) + 1 for grade in range(2, count + 1)]
    rest, given = total - limit - (count - 1), [1] * (count - 1)
    while rest > 0:
        free = [i for i in range(count - 1) if given[i] < limit]
        whole, left = sum([loads[i] for i in free]), rest
        for i in free:
            extra = min(limit - given[i], max(1, left * loads[i] // whole), rest)
            given[i] = given[i] + extra
            rest = rest - extra
    return np.array([limit] + given)


def ragged(own_key, count, total, reach, skew):
    if count == 2:
        one = jax.random.randint(own_key, (), max(1, total - reach), min(reach, total - 1) + 1)
        return jnp.stack([one, total - one])
    tallies = jnp.asarray(length_profile(count, total, reach, skew), jnp.int32)
    couples = (count - 1) // 2
    giver, sink = tallies[1:1 + 2 * couples:2], tallies[2:2 + 2 * couples:2]
    margin = jnp.minimum(giver - 1, reach - sink)
    moved = jax.random.randint(jax.random.fold_in(own_key, 1), (couples,), 0, 1 << 20) % (margin + 1)
    tallies = tallies.at[1:1 + 2 * couples:2].set(giver - moved).at[2:2 + 2 * couples:2].set(sink + moved)
    return tallies[jax.random.permutation(jax.random.fold_in(own_key, 2), count)]


def centred(key, extent, width, limit, shards=(), held_as=jnp.bfloat16):
    entries = width * jax.random.normal(key, extent, jnp.float32)
    if shards:
        entries = entries * levels(key, extent, shards, -0.22, 0.18)
    return jnp.clip(entries, -limit, limit).astype(held_as)


def setup_inputs(seed: int = 0) -> dict:
    splits = jax.random.split(jax.random.key(seed), 16)
    return {
        "tokens": centred(splits[0], (TOKENS, D), 1.0, 6.0, ((0, 32), (1, 16))),
        "norm_gain": jnp.clip(1.0 + 0.18 * jax.random.normal(splits[1], (D,), jnp.float32), 0.1, 1.9),
        "doc_lengths": jax.vmap(lambda own: ragged(own, DOCS, TOK_DEV, TOK_DEV // 2, 2))(jax.random.split(splits[2], N_POOL)).reshape((N_POOL, DOCS)).astype(jnp.int32),
        "query_master": draw_query_master(jax.random.fold_in(splits[15], 71), 0),
        "query_grad": centred(splits[4], (D, QW), 2.0, 12.0, ((0, 32), (1, 16))),
        "query_first": centred(splits[5], (D, QW), 1.0, 6.0, ((0, 32), (1, 16)), jnp.float32),
        "query_second": jnp.clip(jnp.exp(math.log(4.0) - 3.6888794 * jax.random.uniform(splits[6], (D, QW), jnp.float32) ** levels(splits[6], (D, QW), ((0, 32), (1, 16)), -0.2, 0.2)), 0.1, 4.0),
        "kv_master": draw_kv_master(jax.random.fold_in(splits[15], 71), 0),
        "kv_grad": centred(splits[8], (2, D, KVW), 2.0, 12.0, ((1, 32), (2, 16))),
        "kv_first": centred(splits[9], (2, D, KVW), 1.0, 6.0, ((1, 32), (2, 16)), jnp.float32),
        "kv_second": jnp.clip(jnp.exp(math.log(4.0) - 3.6888794 * jax.random.uniform(splits[10], (2, D, KVW), jnp.float32) ** levels(splits[10], (2, D, KVW), ((1, 32), (2, 16)), -0.2, 0.2)), 0.1, 4.0),
        "out_master": centred(splits[11], (QW, D), QW ** -0.5, 0.09375, ((0, 512),), jnp.float32),
        "out_grad": centred(splits[12], (QW, D), 2.0, 12.0, ((0, 512),)),
        "out_first": centred(splits[13], (QW, D), 1.0, 6.0, ((0, 512),), jnp.float32),
        "out_second": jnp.clip(jnp.exp(math.log(4.0) - 3.6888794 * jax.random.uniform(splits[14], (QW, D), jnp.float32) ** levels(splits[14], (QW, D), ((0, 512),), -0.2, 0.2)), 0.1, 4.0),
    }


beta_first = 0.9
beta_second = 0.95
learn_rate = 0.001
adam_eps = 1e-08
norm_eps = 1e-06

def adam_step(master, gradient, first, second):
    grad_value = gradient.astype(jnp.float32)
    first = beta_first * first + (1.0 - beta_first) * grad_value
    second = beta_second * second + (1.0 - beta_second) * grad_value * grad_value
    correct_first = 1.0 - beta_first ** 10
    correct_second = 1.0 - beta_second ** 10
    master = master - learn_rate * (first / correct_first) / (jnp.sqrt(second / correct_second) + adam_eps)
    return (master, first, second, master.astype(jnp.bfloat16))

def reference(tokens, norm_gain, doc_lengths, query_master, query_grad, query_first, query_second, kv_master, kv_grad, kv_first, kv_second, out_master, out_grad, out_first, out_second):
    q_master, q_first, q_second, q_weight = adam_step(query_master, query_grad, query_first, query_second)
    k_master, k_first, k_second, k_weight = adam_step(kv_master, kv_grad, kv_first, kv_second)
    o_master, o_first, o_second, o_weight = adam_step(out_master, out_grad, out_first, out_second)
    values_in = tokens.astype(jnp.float32)
    scale = lax.rsqrt(lax.optimization_barrier(jnp.mean(values_in * values_in, axis=-1, keepdims=True)) + norm_eps)
    normed = (values_in * scale * norm_gain.astype(jnp.float32)).astype(jnp.bfloat16)
    query = jnp.dot(normed, q_weight, preferred_element_type=jnp.float32).astype(jnp.bfloat16)
    keys = jnp.dot(normed, k_weight[0], preferred_element_type=jnp.float32).astype(jnp.bfloat16)
    values = jnp.dot(normed, k_weight[1], preferred_element_type=jnp.float32).astype(jnp.bfloat16)
    share = HEADS // KV_HEADS
    query_groups = query.reshape(N_POOL, TOK_DEV, HEADS, HEAD_DIM)
    key_groups = keys.reshape(N_POOL, TOK_DEV, KV_HEADS, HEAD_DIM)
    value_groups = values.reshape(N_POOL, TOK_DEV, KV_HEADS, HEAD_DIM)

    def attend(items):
        q_block, k_block, v_block, lengths = items
        ends = jnp.cumsum(lengths.astype(jnp.int32)).astype(jnp.int32)
        positions = jnp.arange(TOK_DEV, dtype=jnp.int32)
        segment = lax.optimization_barrier(jnp.sum((ends[None, :] <= positions[:, None]).astype(jnp.int32), axis=1))
        allowed = (segment[:, None] == segment[None, :]) & (positions[None, :] <= positions[:, None])
        k_full = jnp.tile(k_block, (1, share, 1)).astype(jnp.float32)
        v_full = jnp.tile(v_block, (1, share, 1)).astype(jnp.float32)
        scores = jnp.einsum('thd,shd->hts', q_block.astype(jnp.float32), k_full) * HEAD_DIM ** (-0.5)
        scores = jnp.where(allowed[None], scores, -1e+30)
        scores = scores - lax.optimization_barrier(jnp.max(scores, axis=-1, keepdims=True))
        weights = jnp.exp(scores)
        weights = (weights / lax.optimization_barrier(jnp.sum(weights, axis=-1, keepdims=True))).astype(jnp.bfloat16)
        context = jnp.einsum('hts,shd->thd', weights.astype(jnp.float32), v_full)
        return context.astype(jnp.bfloat16).reshape(TOK_DEV, QW)
    context = lax.map(attend, (query_groups, key_groups, value_groups, doc_lengths)).reshape(TOKENS, QW)
    group_width = QW // N_TP
    context_parts = context.reshape(TOKENS, N_TP, group_width).transpose(1, 0, 2)
    out_parts = o_weight.reshape(N_TP, group_width, D)

    def accumulate(total, items):
        part_context, part_weight = items
        term = jnp.dot(part_context, part_weight, preferred_element_type=jnp.float32).astype(jnp.bfloat16)
        term = lax.optimization_barrier(term)
        return (total + term.astype(jnp.float32), None)
    total, _ = lax.scan(accumulate, jnp.zeros((TOKENS, D), jnp.float32), (context_parts, out_parts))
    mixed = total.astype(jnp.bfloat16)
    return (mixed, q_master, q_first, q_second, k_master, k_first, k_second, o_master, o_first, o_second)
```

```python
import jax
import jax.numpy as jnp
from jax import lax
from jax.experimental import pallas as pl
from jax.experimental.pallas import tpu as pltpu
from jax.sharding import Mesh, PartitionSpec as P

HEAD_DIM = 128
ROWS = 192
MIB = 1 << 20

beta_first = 0.9
beta_second = 0.95
learn_rate = 0.001
adam_eps = 1e-08
norm_eps = 1e-06

STEPS = (4, 2, 1)
ORDER = (0, 4, 2, 6, 1, 5, 3, 7)


def adam_step(master, gradient, first, second):
    grad_value = gradient.astype(jnp.float32)
    first = beta_first * first + (1.0 - beta_first) * grad_value
    second = beta_second * second + (1.0 - beta_second) * grad_value * grad_value
    correct_first = 1.0 - beta_first**10
    correct_second = 1.0 - beta_second**10
    master = master - learn_rate * (first / correct_first) / (
        jnp.sqrt(second / correct_second) + adam_eps
    )
    return (master, first, second, master.astype(jnp.bfloat16))


def swap_z(value, bit):
    return lax.ppermute(value, "z", [(z, z ^ bit) for z in range(8)])


def swap_core(value):
    return lax.ppermute(value, "c", [(0, 1), (1, 0)])


def swap_half(value):
    return lax.ppermute(value, "h", [(0, 1), (1, 0)])


def gather_plane(value):
    whole = jnp.broadcast_to(value[None], (16,) + value.shape)
    return lax.all_to_all(whole, ("x", "y"), 0, 0, tiled=True)


def vmem(count):
    return [pl.BlockSpec(memory_space=pltpu.VMEM)] * count


def smem():
    return pl.BlockSpec(memory_space=pltpu.SMEM)


def params(mib):
    return pltpu.CompilerParams(vmem_limit_bytes=mib * MIB)


def norm_kernel(place, gain, near, far, core_near, core_far, out):
    z, c = place[0], place[1]
    blocks = []
    for other, pair in enumerate(((near, far), (core_near, core_far))):
        for at in range(8):
            blocks.append((other, at, pair[at // 4], at % 4))

    def chunk(i, carry):
        rows = pl.ds(pl.multiple_of(i * 16, 16), 16)
        total = jnp.zeros((16, 512), jnp.float32)
        for _, _, ref, at in blocks:
            value = ref[at, rows, :].astype(jnp.float32)
            total = total + value * value
        mean = jnp.sum(total, axis=-1, keepdims=True) * (1.0 / 8192)
        scale = lax.rsqrt(mean + norm_eps)
        for other, place_at, ref, at in blocks:
            value = ref[at, rows, :].astype(jnp.float32)
            features = (z ^ ORDER[place_at]) * 2 + (c ^ other)
            value = value * scale * gain[features]
            out[other, place_at, rows, :] = value.astype(jnp.bfloat16)
        return carry

    lax.fori_loop(0, ROWS // 16, chunk, 0)


def norm_tokens(place, gain, near, far, core_near, core_far):
    return pl.pallas_call(
        norm_kernel,
        out_shape=jax.ShapeDtypeStruct((2, 8, ROWS, 512), jnp.bfloat16),
        in_specs=[smem()] + vmem(5),
        out_specs=vmem(1)[0],
        compiler_params=params(24),
        cost_estimate=pl.CostEstimate(
            flops=8 * ROWS * 8192, bytes_accessed=6 * MIB, transcendentals=0
        ),
        name="norm_tokens",
    )(place, gain, near, far, core_near, core_far)


def feature_block(place, normed, x, y, slot):
    z, c, h = place[0], place[1], place[2]
    z_rel = (x * 2 + (slot ^ h)) ^ z
    at = ((z_rel & 1) * 4) | (z_rel & 2) | (z_rel // 4)
    return normed[(y // 2) ^ c, at, :, (y % 2) * 256 : (y % 2) * 256 + 256]


def kv_kernel(place, normed, weight, out):
    total = jnp.zeros((64, ROWS), jnp.float32)
    for x in range(4):
        for y in range(4):
            for slot in range(2):
                total = total + lax.dot_general(
                    weight[x * 4 + y, slot],
                    feature_block(place, normed, x, y, slot),
                    (((1,), (1,)), ((), ())),
                    preferred_element_type=jnp.float32,
                )
    out[...] = total.astype(jnp.bfloat16)


def project_kv(place, normed, weight):
    return pl.pallas_call(
        kv_kernel,
        out_shape=jax.ShapeDtypeStruct((64, ROWS), jnp.bfloat16),
        in_specs=[smem()] + vmem(2),
        out_specs=vmem(1)[0],
        compiler_params=params(16),
        cost_estimate=pl.CostEstimate(
            flops=2 * ROWS * 8192 * 64, bytes_accessed=4 * MIB, transcendentals=0
        ),
        name="project_kv",
    )(place, normed, weight)


def query_kernel(place, normed, weight, out, total):
    step = pl.program_id(0)

    @pl.when(step == 0)
    def _():
        total[...] = jnp.zeros_like(total)

    part = jnp.zeros((ROWS, 256), jnp.float32)
    for y in range(4):
        for slot in range(2):
            part = part + jnp.dot(
                feature_block(place, normed, step, y, slot),
                weight[y, slot],
                preferred_element_type=jnp.float32,
            )
    total[...] += part

    @pl.when(step == 3)
    def _():
        out[...] = total[...].astype(jnp.bfloat16)


def project_query(place, normed, weight):
    return pl.pallas_call(
        query_kernel,
        grid=(4,),
        out_shape=jax.ShapeDtypeStruct((ROWS, 256), jnp.bfloat16),
        in_specs=[
            smem(),
            pl.BlockSpec((2, 8, ROWS, 512), lambda i: (0, 0, 0, 0)),
            pl.BlockSpec((4, 2, 256, 256), lambda i: (i, 0, 0, 0)),
        ],
        out_specs=pl.BlockSpec((ROWS, 256), lambda i: (0, 0)),
        scratch_shapes=[pltpu.VMEM((ROWS, 256), jnp.float32)],
        compiler_params=params(24),
        cost_estimate=pl.CostEstimate(
            flops=2 * ROWS * 8192 * 256, bytes_accessed=7 * MIB, transcendentals=0
        ),
        name="project_query",
    )(place, normed, weight)


def attend_kernel(place, lengths, query, pieces, out, held):
    z = place[0]
    for at in range(8):
        held[z ^ ORDER[at]] = pieces[at]
    query_at = lax.broadcasted_iota(jnp.int32, (ROWS, ROWS), 0)
    key_at = lax.broadcasted_iota(jnp.int32, (ROWS, ROWS), 1)
    query_doc = jnp.zeros((ROWS, ROWS), jnp.int32)
    key_doc = jnp.zeros((ROWS, ROWS), jnp.int32)
    end = 0
    for doc in range(4):
        end = end + lengths[0, doc]
        query_doc = query_doc + (query_at >= end).astype(jnp.int32)
        key_doc = key_doc + (key_at >= end).astype(jnp.int32)
    allowed = (query_doc == key_doc) & (key_at <= query_at)
    for head in range(2):
        keys = held[head * 4 : head * 4 + 4, 0:32, :].reshape(HEAD_DIM, ROWS)
        values = held[head * 4 : head * 4 + 4, 32:64, :].reshape(HEAD_DIM, ROWS)
        columns = slice(head * HEAD_DIM, (head + 1) * HEAD_DIM)
        scores = jnp.dot(query[:, columns], keys, preferred_element_type=jnp.float32)
        scores = jnp.where(allowed, scores * HEAD_DIM**-0.5, -1e30)
        scores = scores - jnp.max(scores, axis=-1, keepdims=True)
        weights = jnp.exp(scores)
        weights = weights / jnp.sum(weights, axis=-1, keepdims=True)
        context = lax.dot_general(
            weights.astype(jnp.bfloat16),
            values,
            (((1,), (1,)), ((), ())),
            preferred_element_type=jnp.float32,
        )
        out[:, columns] = context.astype(jnp.bfloat16)


def attend(place, lengths, query, pieces):
    return pl.pallas_call(
        attend_kernel,
        out_shape=jax.ShapeDtypeStruct((ROWS, 256), jnp.bfloat16),
        in_specs=[smem(), smem()] + vmem(2),
        out_specs=vmem(1)[0],
        scratch_shapes=[pltpu.VMEM((8, 64, ROWS), jnp.bfloat16)],
        compiler_params=params(16),
        cost_estimate=pl.CostEstimate(
            flops=8 * ROWS * ROWS * HEAD_DIM,
            bytes_accessed=MIB // 2,
            transcendentals=2 * ROWS * ROWS,
        ),
        name="attend",
    )(place, lengths, query, pieces)


def output_kernel(place, near, far, weight, out, *, other):
    z, c = place[0], place[1]
    start = pl.multiple_of((c ^ other) * 512, 512)
    total = jnp.zeros((ROWS, 512), jnp.float32)
    for at in range(8):
        part = (near if at < 4 else far)[at % 4]
        total = total + jnp.dot(
            part,
            weight[z ^ ORDER[at], :, pl.ds(start, 512)],
            preferred_element_type=jnp.float32,
        )
    out[...] = total.astype(out.dtype)


def project_output(place, near, far, weight, other):
    def kernel(*refs):
        output_kernel(*refs, other=other)

    return pl.pallas_call(
        kernel,
        out_shape=jax.ShapeDtypeStruct(
            (ROWS, 512), jnp.bfloat16 if other else jnp.float32
        ),
        in_specs=[smem()] + vmem(3),
        out_specs=vmem(1)[0],
        compiler_params=params(24),
        cost_estimate=pl.CostEstimate(
            flops=2 * ROWS * 2048 * 512, bytes_accessed=5 * MIB, transcendentals=0
        ),
        name="output_other" if other else "output_own",
    )(place, near, far, weight)


def rotate(index):
    return ((index * 2) & 15) | (index // 8)


def shards(
    tokens,
    norm_gain,
    doc_lengths,
    query_master,
    query_grad,
    query_first,
    query_second,
    kv_master,
    kv_grad,
    kv_first,
    kv_second,
    out_master,
    out_grad,
    out_first,
    out_second,
):
    h = lax.axis_index("h")
    place = jnp.stack([lax.axis_index("z"), lax.axis_index("c"), h]).astype(jnp.int32)

    with jax.named_scope("tokens"):
        near = tokens[None]
        for bit in STEPS[:2]:
            near = jnp.concatenate([near, swap_z(near, bit)])
        far = swap_z(near, STEPS[2])
        core_near = swap_core(near)
        core_far = swap_core(far)

    with jax.named_scope("adam"):
        q_master, q_first, q_second, q_weight = adam_step(
            query_master, query_grad, query_first, query_second
        )
        k_master, k_first, k_second, k_weight = adam_step(
            kv_master, kv_grad, kv_first, kv_second
        )
        o_master, o_first, o_second, o_weight = adam_step(
            out_master, out_grad, out_first, out_second
        )

    with jax.named_scope("kv_weight"):
        k_rows = k_weight.transpose(0, 2, 1).reshape(64, 256)
        own = lax.ppermute(k_rows, ("z", "c"), [(i, rotate(i)) for i in range(16)])
        crossed = lax.ppermute(
            k_rows,
            ("h", "z", "c"),
            [(i * 16 + j, (1 - i) * 16 + rotate(j)) for i in range(2) for j in range(16)],
        )
        kv_whole = gather_plane(jnp.stack([own, crossed]))

    with jax.named_scope("query_weight"):
        q_whole = gather_plane(jnp.stack([q_weight, swap_half(q_weight)]))

    with jax.named_scope("out_weight"):
        o_parts = o_weight.reshape(8, 8, 1024).transpose(1, 0, 2)
        o_parts = lax.all_to_all(o_parts, "z", 0, 0, tiled=True)
        o_crossed = swap_half(o_parts)
        o_halves = jnp.where(
            h == 0, jnp.stack([o_parts, o_crossed]), jnp.stack([o_crossed, o_parts])
        )
        o_whole = lax.all_gather(o_halves, ("x", "y"), axis=0, tiled=False)
        o_whole = o_whole.reshape(4, 4, 2, 8, 8, 1024).transpose(3, 0, 2, 1, 4, 5)
        o_whole = o_whole.reshape(8, 256, 1024)

    with jax.named_scope("projections"):
        gain = norm_gain.reshape(16, 1, 512)
        normed = norm_tokens(place, gain, near, far, core_near, core_far)
        pieces = project_kv(place, normed, kv_whole)[None]
        for bit in STEPS:
            pieces = jnp.concatenate([pieces, swap_z(pieces, bit)])
        query = project_query(place, normed, q_whole)

    with jax.named_scope("attention"):
        context = attend(place, doc_lengths, query, pieces)[None]
        for bit in STEPS[:2]:
            context = jnp.concatenate([context, swap_z(context, bit)])
        context_far = swap_z(context, STEPS[2])

    with jax.named_scope("output"):
        sent = swap_core(project_output(place, context, context_far, o_whole, 1))
        kept = project_output(place, context, context_far, o_whole, 0)
        mixed = (kept + sent.astype(jnp.float32)).astype(jnp.bfloat16)

    return (
        mixed,
        q_master,
        q_first,
        q_second,
        k_master,
        k_first,
        k_second,
        o_master,
        o_first,
        o_second,
    )


def solution(mesh):
    pool, tp = ("x", "h", "y"), ("z", "c")
    split = Mesh(mesh.devices.reshape(4, 2, 4, 8, 2), ("x", "h", "y", "z", "c"))
    weight = P(pool, tp)
    kv_weight = P(None, pool, tp)
    out_weight = P(tp + pool, None)
    in_specs = (
        (P(pool, tp), P(), P(pool, None))
        + (weight,) * 4
        + (kv_weight,) * 4
        + (out_weight,) * 4
    )
    out_specs = (P(pool, tp),) + (weight,) * 3 + (kv_weight,) * 3 + (out_weight,) * 3
    return jax.shard_map(
        shards, mesh=split, in_specs=in_specs, out_specs=out_specs, check_vma=False
    )
```

```python
import jax
import jax.numpy as jnp
from jax import lax
from jax.experimental import pallas as pl
from jax.experimental.pallas import tpu as pltpu
from jax.sharding import Mesh, PartitionSpec as P

HEAD_DIM = 128
ROWS = 192
LANES = 256
MIB = 1 << 20

beta_first = 0.9
beta_second = 0.95
learn_rate = 0.001
adam_eps = 1e-08
norm_eps = 1e-06

ORDER = (0, 4, 2, 6, 1, 5, 3, 7)
BLOCK = (0, 2, 1, 3)

Q_ROWS, KV_ROWS, SUM_ROWS = 192, 64, 16
PART_ROWS = Q_ROWS + KV_ROWS + SUM_ROWS


def adam_step(master, gradient, first, second):
    grad_value = gradient.astype(jnp.float32)
    first = beta_first * first + (1.0 - beta_first) * grad_value
    second = beta_second * second + (1.0 - beta_second) * grad_value * grad_value
    correct_first = 1.0 - beta_first**10
    correct_second = 1.0 - beta_second**10
    master = master - learn_rate * (first / correct_first) / (
        jnp.sqrt(second / correct_second) + adam_eps
    )
    return (master, first, second, master.astype(jnp.bfloat16))


def swap_z(value, bit):
    return lax.ppermute(value, "z", [(z, z ^ bit) for z in range(8)])


def swap_core(value):
    return lax.ppermute(value, "c", [(0, 1), (1, 0)])


def gather_line(pair):
    return [pair] + [swap_z(pair, step) for step in (2, 1, 3)]


def swap_corner(value):
    moves = [(z * 2 + c, (z ^ 4) * 2 + (c ^ 1)) for z in range(8) for c in range(2)]
    return lax.ppermute(value, ("z", "c"), moves)


def swap_bits(value, other_half):
    moves = []
    for x in range(4):
        for h in range(2):
            for y in range(4):
                for z in range(8):
                    for c in range(2):
                        to_x, to_z = (z // 4) * 2 + x % 2, (x // 2) * 4 + z % 4
                        source = (((x * 2 + h) * 4 + y) * 8 + z) * 2 + c
                        half = h ^ other_half
                        target = (((to_x * 2 + half) * 4 + y) * 8 + to_z) * 2 + c
                        moves.append((source, target))
    return lax.ppermute(value, ("x", "h", "y", "z", "c"), moves)


def spread_groups(tokens, y):
    halves = tokens.reshape(ROWS, 2, LANES).transpose(1, 0, 2)
    got = []
    for turn in range(2):
        moves = []
        for at in range(4):
            for c in range(2):
                block = (at % 2) ^ turn
                moves.append((at * 2 + c, (c * 2 + block) * 2 + at // 2))
        piece = jnp.where(y % 2 == 0, halves[turn], halves[1 - turn])
        got.append(lax.ppermute(piece, ("y", "c"), moves))
    return jnp.stack(got)


def gather_columns(value):
    whole = jnp.broadcast_to(value[None], (4,) + value.shape)
    return lax.all_to_all(whole, "x", 0, 0, tiled=True)


def after(value, *others):
    return lax.optimization_barrier((value,) + others)[0]


def vmem(count):
    return [pl.BlockSpec(memory_space=pltpu.VMEM)] * count


def smem():
    return pl.BlockSpec(memory_space=pltpu.SMEM)


def params(mib):
    return pltpu.CompilerParams(vmem_limit_bytes=mib * MIB)


def lanes_of(column):
    wide = jnp.broadcast_to(column, (ROWS, 128))
    wide = jnp.concatenate([wide, jnp.zeros((LANES - ROWS, 128), jnp.float32)])
    return wide.T[0:8]


def split_sum(rows):
    high = rows.astype(jnp.bfloat16)
    low = (rows - high.astype(jnp.float32)).astype(jnp.bfloat16)
    return jnp.concatenate([high, low])


def join_sum(rows):
    rows = rows.astype(jnp.float32)
    return rows[0:8] + rows[8:16]


def gain_kernel(place, gain, own, rest, core_own, core_rest, out, sums):
    z, y = place[0], place[3]
    for other, (first, others) in enumerate(((own, rest), (core_own, core_rest))):
        for turn in range(2):
            total = jnp.zeros((ROWS, LANES), jnp.float32)
            for at in range(4):
                value = first[turn] if at == 0 else others[at - 1, turn]
                value = value.astype(jnp.float32)
                total = total + value * value
                value = value * gain[(z ^ BLOCK[at]) * 4 + y]
                rows = pl.ds((other * 2 + turn) * ROWS, ROWS)
                out[at, rows, :] = value.astype(jnp.bfloat16)
            column = jnp.sum(total, axis=-1, keepdims=True)
            sums[other * 2 + turn] = split_sum(lanes_of(column))


def apply_gain(place, gain, own, rest, core_own, core_rest):
    return pl.pallas_call(
        gain_kernel,
        out_shape=(
            jax.ShapeDtypeStruct((4, 4 * ROWS, LANES), jnp.bfloat16),
            jax.ShapeDtypeStruct((4, SUM_ROWS, LANES), jnp.bfloat16),
        ),
        in_specs=[smem()] + vmem(5),
        out_specs=tuple(vmem(2)),
        compiler_params=params(12),
        cost_estimate=pl.CostEstimate(
            flops=4 * ROWS * 4096, bytes_accessed=3 * MIB, transcendentals=0
        ),
        name="apply_gain",
    )(place, gain, own, rest, core_own, core_rest)


def project_kernel(place, scaled, sums, weight, out):
    z, c, h, y = place[0], place[1], place[2], place[3]
    blocks = []
    for x in range(2):
        for slot in range(2):
            step = (x * 2 + (slot ^ h)) ^ (z & 3)
            blocks.append((x, slot, ((step & 1) * 2) | (step // 2)))
    query = jnp.zeros((4 * ROWS, LANES), jnp.float32)
    for x, slot, at in blocks:
        query = query + jnp.dot(
            scaled[at], weight[x, slot, 0:256, :], preferred_element_type=jnp.float32
        )
    for other in range(2):
        for turn in range(2):
            place_in = other * 2 + turn
            rows = slice(place_in * ROWS, (place_in + 1) * ROWS)
            group = (c ^ other) * 2 + ((y & 1) ^ turn)
            out[group, 0, 0:Q_ROWS, :] = query[rows].astype(jnp.bfloat16)
            total = jnp.zeros((KV_ROWS, ROWS), jnp.float32)
            for x, slot, at in blocks:
                total = total + lax.dot_general(
                    weight[x, slot, 256:320, :],
                    scaled[at, rows, :],
                    (((1,), (1,)), ((), ())),
                    preferred_element_type=jnp.float32,
                )
            total = jnp.concatenate(
                [total, jnp.zeros((KV_ROWS, LANES - ROWS), jnp.float32)], axis=1
            )
            out[group, 0, Q_ROWS : Q_ROWS + KV_ROWS, :] = total.astype(jnp.bfloat16)
            out[group, 0, Q_ROWS + KV_ROWS : PART_ROWS, :] = sums[place_in]


def project(place, scaled, sums, weight):
    return pl.pallas_call(
        project_kernel,
        grid=(2,),
        out_shape=jax.ShapeDtypeStruct((4, 2, PART_ROWS, LANES), jnp.bfloat16),
        in_specs=[
            smem(),
            pl.BlockSpec((4, 4 * ROWS, LANES), lambda i: (0, 0, 0)),
            pl.BlockSpec((4, SUM_ROWS, LANES), lambda i: (0, 0, 0)),
            pl.BlockSpec((2, 2, 320, LANES), lambda i: (i, 0, 0, 0)),
        ],
        out_specs=pl.BlockSpec((4, 1, PART_ROWS, LANES), lambda i: (0, i, 0, 0)),
        compiler_params=params(20),
        cost_estimate=pl.CostEstimate(
            flops=2 * ROWS * 8192 * 320, bytes_accessed=4 * MIB, transcendentals=0
        ),
        name="project",
    )(place, scaled, sums, weight)


def reduce_kernel(place, parts, query, sums, sent, kv_same, kv_other):
    high, c = place[0] // 4, place[1]

    def total(group, start, rows):
        value = jnp.zeros((rows, LANES), jnp.float32)
        for source in range(4):
            value = value + parts[source, group, start : start + rows, :].astype(
                jnp.float32
            )
        return value

    query[...] = total(high, 0, Q_ROWS)
    sent[0:Q_ROWS, :] = total(1 - high, 0, Q_ROWS).astype(jnp.bfloat16)
    squares = join_sum(total(0, Q_ROWS + KV_ROWS, SUM_ROWS))
    sums[...] = squares
    sent[Q_ROWS : Q_ROWS + SUM_ROWS, :] = split_sum(squares)
    kv_same[...] = total(c, Q_ROWS, KV_ROWS).astype(jnp.bfloat16)
    kv_other[...] = total(1 - c, Q_ROWS, KV_ROWS).astype(jnp.bfloat16)


def reduce_parts(place, parts):
    return pl.pallas_call(
        reduce_kernel,
        out_shape=(
            jax.ShapeDtypeStruct((Q_ROWS, LANES), jnp.float32),
            jax.ShapeDtypeStruct((8, LANES), jnp.float32),
            jax.ShapeDtypeStruct((Q_ROWS + SUM_ROWS, LANES), jnp.bfloat16),
            jax.ShapeDtypeStruct((KV_ROWS, LANES), jnp.bfloat16),
            jax.ShapeDtypeStruct((KV_ROWS, LANES), jnp.bfloat16),
        ),
        in_specs=[smem()] + vmem(1),
        out_specs=tuple(vmem(5)),
        compiler_params=params(8),
        cost_estimate=pl.CostEstimate(
            flops=4 * MIB, bytes_accessed=2 * MIB, transcendentals=0
        ),
        name="reduce_parts",
    )(place, parts)


def attend_kernel(
    place, lengths, query, sums, got, p0, p2, p1, p3, out, held
):
    z, c = place[0], place[1]
    squares = sums[...] + join_sum(got[Q_ROWS : Q_ROWS + SUM_ROWS, :])
    scale = lax.rsqrt(squares * (1.0 / 8192) + norm_eps)[0:1, :]
    for step, pair in ((0, p0), (2, p2), (1, p1), (3, p3)):
        for at in range(2):
            piece = pair[at].astype(jnp.float32) * scale
            held[((z & 3) ^ step) * 2 + (c ^ at)] = piece.astype(jnp.bfloat16)
    column = jnp.broadcast_to(scale, (128, LANES)).T[0:ROWS, 0:1]
    heads = query[...] + got[0:Q_ROWS, :].astype(jnp.float32)
    heads = (heads * column).astype(jnp.bfloat16)
    query_at = lax.broadcasted_iota(jnp.int32, (ROWS, LANES), 0)
    key_at = lax.broadcasted_iota(jnp.int32, (ROWS, LANES), 1)
    query_doc = jnp.zeros((ROWS, LANES), jnp.int32)
    key_doc = jnp.zeros((ROWS, LANES), jnp.int32)
    end = 0
    for doc in range(4):
        end = end + lengths[0, doc]
        query_doc = query_doc + (query_at >= end).astype(jnp.int32)
        key_doc = key_doc + (key_at >= end).astype(jnp.int32)
    allowed = (query_doc == key_doc) & (key_at <= query_at)
    for head in range(2):
        keys = held[head * 4 : head * 4 + 4, 0:32, :].reshape(HEAD_DIM, LANES)
        values = held[head * 4 : head * 4 + 4, 32:64, :].reshape(HEAD_DIM, LANES)
        columns = slice(head * HEAD_DIM, (head + 1) * HEAD_DIM)
        scores = jnp.dot(heads[:, columns], keys, preferred_element_type=jnp.float32)
        scores = jnp.where(allowed, scores * HEAD_DIM**-0.5, -1e30)
        scores = scores - jnp.max(scores, axis=-1, keepdims=True)
        weights = jnp.exp(scores)
        weights = weights / jnp.sum(weights, axis=-1, keepdims=True)
        context = lax.dot_general(
            weights.astype(jnp.bfloat16),
            values,
            (((1,), (1,)), ((), ())),
            preferred_element_type=jnp.float32,
        )
        out[:, columns] = context.astype(jnp.bfloat16)


def attend(place, lengths, query, sums, got, pairs):
    return pl.pallas_call(
        attend_kernel,
        out_shape=jax.ShapeDtypeStruct((ROWS, 256), jnp.bfloat16),
        in_specs=[smem(), smem()] + vmem(7),
        out_specs=vmem(1)[0],
        scratch_shapes=[pltpu.VMEM((8, KV_ROWS, LANES), jnp.bfloat16)],
        compiler_params=params(8),
        cost_estimate=pl.CostEstimate(
            flops=8 * ROWS * ROWS * HEAD_DIM,
            bytes_accessed=MIB // 2,
            transcendentals=2 * ROWS * ROWS,
        ),
        name="attend",
    )(place, lengths, query, sums, got, *pairs)


def output_kernel(place, p0, p2, p1, p3, weight, out, *, other):
    start = pl.multiple_of((place[1] ^ other) * 512, 512)
    total = jnp.zeros((ROWS, 512), jnp.float32)
    for at in range(8):
        part = (p0, p2, p1, p3)[at // 2][at % 2]
        total = total + jnp.dot(
            part,
            weight[place[0] ^ ORDER[at], :, pl.ds(start, 512)],
            preferred_element_type=jnp.float32,
        )
    out[...] = total.astype(out.dtype)


def project_output(place, pairs, weight, other):
    def kernel(*refs):
        output_kernel(*refs, other=other)

    return pl.pallas_call(
        kernel,
        out_shape=jax.ShapeDtypeStruct(
            (ROWS, 512), jnp.bfloat16 if other else jnp.float32
        ),
        in_specs=[smem()] + vmem(5),
        out_specs=vmem(1)[0],
        compiler_params=params(24),
        cost_estimate=pl.CostEstimate(
            flops=2 * ROWS * 2048 * 512, bytes_accessed=5 * MIB, transcendentals=0
        ),
        name="output_other" if other else "output_own",
    )(place, *pairs, weight)


def shards(
    tokens,
    norm_gain,
    doc_lengths,
    query_master,
    query_grad,
    query_first,
    query_second,
    kv_master,
    kv_grad,
    kv_first,
    kv_second,
    out_master,
    out_grad,
    out_first,
    out_second,
):
    z, c, h, y = (lax.axis_index(name) for name in ("z", "c", "h", "y"))
    place = jnp.stack([z, c, h, y]).astype(jnp.int32)

    with jax.named_scope("adam"):
        q_master, q_first, q_second, q_weight = adam_step(
            query_master, query_grad, query_first, query_second
        )
        k_master, k_first, k_second, k_weight = adam_step(
            kv_master, kv_grad, kv_first, kv_second
        )
        o_master, o_first, o_second, o_weight = adam_step(
            out_master, out_grad, out_first, out_second
        )

    with jax.named_scope("in_weight"):
        k_rows = k_weight.transpose(0, 2, 1).reshape(KV_ROWS, 256)
        w_rows = jnp.concatenate([q_weight, k_rows])
        w_rows = jnp.stack([swap_bits(w_rows, 0), swap_bits(w_rows, 1)])
        w_whole = gather_columns(w_rows)

    with jax.named_scope("tokens"):
        own = spread_groups(tokens, y)
        core_own = swap_core(own)
        rest = jnp.stack([swap_z(own, step) for step in BLOCK[1:]])
        core_rest = swap_core(rest)
        gain = norm_gain.reshape(32, 1, LANES)
        scaled, sums = apply_gain(place, gain, own, rest, core_own, core_rest)

    with jax.named_scope("out_columns"):
        o_parts = o_weight.reshape(8, 8, 1024).transpose(1, 0, 2)
        o_parts = jnp.broadcast_to(o_parts[None], (2, 8, 8, 1024)).reshape(16, 8, 1024)
        o_parts = lax.all_to_all(o_parts, ("h", "z"), 0, 0, tiled=True)
        o_halves = o_parts.reshape(2, 8, 8, 1024)

    with jax.named_scope("out_weight"):
        o_whole = lax.all_gather(o_halves, ("x", "y"), axis=0, tiled=False)
        o_whole = o_whole.reshape(4, 4, 2, 8, 8, 1024).transpose(3, 0, 2, 1, 4, 5)
        o_whole = o_whole.reshape(8, 256, 1024)

    with jax.named_scope("projections"):
        parts = project(place, scaled, sums, w_whole)
        parts = lax.all_to_all(parts, "y", 0, 0, tiled=True)
        query, sums, sent, kv_same, kv_other = reduce_parts(place, parts)
        same = kv_same.astype(jnp.float32) + swap_z(kv_same, 4).astype(jnp.float32)
        other = swap_core(kv_other).astype(jnp.float32) + swap_corner(
            kv_other
        ).astype(jnp.float32)
        pieces = jnp.stack([same, other]).astype(jnp.bfloat16)
        got = swap_z(after(sent, pieces), 4)
        pieces = gather_line(pieces)

    with jax.named_scope("attention"):
        context = attend(place, doc_lengths, query, sums, got, pieces)
        context = gather_line(jnp.stack([context, swap_z(context, 4)]))

    with jax.named_scope("output"):
        sent = swap_core(project_output(place, context, o_whole, 1))
        kept = project_output(place, context, o_whole, 0)
        mixed = (kept + sent.astype(jnp.float32)).astype(jnp.bfloat16)

    return (
        mixed,
        q_master,
        q_first,
        q_second,
        k_master,
        k_first,
        k_second,
        o_master,
        o_first,
        o_second,
    )


def solution(mesh):
    pool, tp = ("x", "h", "y"), ("z", "c")
    split = Mesh(mesh.devices.reshape(4, 2, 4, 8, 2), ("x", "h", "y", "z", "c"))
    weight = P(pool, tp)
    kv_weight = P(None, pool, tp)
    out_weight = P(tp + pool, None)
    in_specs = (
        (P(pool, tp), P(), P(pool, None))
        + (weight,) * 4
        + (kv_weight,) * 4
        + (out_weight,) * 4
    )
    out_specs = (P(pool, tp),) + (weight,) * 3 + (kv_weight,) * 3 + (out_weight,) * 3
    return jax.shard_map(
        shards, mesh=split, in_specs=in_specs, out_specs=out_specs, check_vma=False
    )
```

```python
import jax
import jax.numpy as jnp
from jax import lax
from jax.experimental import pallas as pl
from jax.experimental.pallas import tpu as pltpu
from jax.sharding import Mesh, PartitionSpec as P

HEAD_DIM = 128
ROWS = 192
LANES = 256
MIB = 1 << 20

beta_first = 0.9
beta_second = 0.95
learn_rate = 0.001
adam_eps = 1e-08
norm_eps = 1e-06

ORDER = (0, 4, 2, 6, 1, 5, 3, 7)
BLOCK = (0, 2, 1, 3)

Q_ROWS, KV_ROWS, SUM_ROWS = 192, 64, 16
KV_START, SUM_START = 2 * Q_ROWS, 2 * Q_ROWS + 2 * KV_ROWS
PART_ROWS = SUM_START + SUM_ROWS


def adam_step(master, gradient, first, second):
    grad_value = gradient.astype(jnp.float32)
    first = beta_first * first + (1.0 - beta_first) * grad_value
    second = beta_second * second + (1.0 - beta_second) * grad_value * grad_value
    correct_first = 1.0 - beta_first**10
    correct_second = 1.0 - beta_second**10
    master = master - learn_rate * (first / correct_first) / (
        jnp.sqrt(second / correct_second) + adam_eps
    )
    return (master, first, second, master.astype(jnp.bfloat16))


def swap_z(value, bit):
    return lax.ppermute(value, "z", [(z, z ^ bit) for z in range(8)])


def swap_core(value):
    return lax.ppermute(value, "c", [(0, 1), (1, 0)])


def gather_line(pair):
    return [pair] + [swap_z(pair, step) for step in (2, 1, 3)]


def swap_line(value, axis, bits):
    return lax.ppermute(value, axis, [(at, at ^ bits) for at in range(4)])


def move_weight(value, flip, turn_core):
    moves = []
    for x in range(4):
        for h in range(2):
            for y in range(4):
                for z in range(8):
                    for c in range(2):
                        to_x, to_c = (c, z // 4) if turn_core else (z // 4, c)
                        to_x, to_z = to_x * 2 + x % 2, (x // 2) * 4 + z % 4
                        source = (((x * 2 + h) * 4 + y) * 8 + z) * 2 + c
                        target = (((to_x * 2 + (h ^ flip)) * 4 + y) * 8 + to_z) * 2
                        moves.append((source, target + to_c))
    return lax.ppermute(value, ("x", "h", "y", "z", "c"), moves)


def spread_groups(tokens, y):
    halves = tokens.reshape(ROWS, 2, LANES).transpose(1, 0, 2)
    got = []
    for turn in range(2):
        moves = []
        for at in range(4):
            for c in range(2):
                block = (at % 2) ^ turn
                moves.append((at * 2 + c, (c * 2 + block) * 2 + at // 2))
        piece = jnp.where(y % 2 == 0, halves[turn], halves[1 - turn])
        got.append(lax.ppermute(piece, ("y", "c"), moves))
    return jnp.stack(got)


def after(value, *others):
    return lax.optimization_barrier((value,) + others)[0]


def vmem(count):
    return [pl.BlockSpec(memory_space=pltpu.VMEM)] * count


def smem():
    return pl.BlockSpec(memory_space=pltpu.SMEM)


def params(mib):
    return pltpu.CompilerParams(vmem_limit_bytes=mib * MIB)


def lanes_of(column):
    wide = jnp.broadcast_to(column, (ROWS, 128))
    wide = jnp.concatenate([wide, jnp.zeros((LANES - ROWS, 128), jnp.float32)])
    return wide.T[0:8]


def split_sum(rows):
    high = rows.astype(jnp.bfloat16)
    low = (rows - high.astype(jnp.float32)).astype(jnp.bfloat16)
    return jnp.concatenate([high, low])


def join_sum(rows):
    rows = rows.astype(jnp.float32)
    return rows[0:8] + rows[8:16]


def gain_kernel(place, gain, own, rest, core_own, core_rest, out, sums):
    z, c, y = place[0], place[1], place[3]
    for other, (first, others) in enumerate(((own, rest), (core_own, core_rest))):
        for turn in range(2):
            group = ((c ^ other) ^ (y // 2)) * 2 + turn
            rows = pl.ds(pl.multiple_of(group * ROWS, ROWS), ROWS)
            total = jnp.zeros((ROWS, LANES), jnp.float32)
            for at in range(4):
                value = first[turn] if at == 0 else others[at - 1, turn]
                value = value.astype(jnp.float32)
                total = total + value * value
                value = value * gain[(z ^ BLOCK[at]) * 4 + y]
                out[at, rows, :] = value.astype(jnp.bfloat16)
            column = jnp.sum(total, axis=-1, keepdims=True)
            sums[group] = split_sum(lanes_of(column))


def apply_gain(place, gain, own, rest, core_own, core_rest):
    return pl.pallas_call(
        gain_kernel,
        out_shape=(
            jax.ShapeDtypeStruct((4, 4 * ROWS, LANES), jnp.bfloat16),
            jax.ShapeDtypeStruct((4, SUM_ROWS, LANES), jnp.bfloat16),
        ),
        in_specs=[smem()] + vmem(5),
        out_specs=tuple(vmem(2)),
        compiler_params=params(12),
        cost_estimate=pl.CostEstimate(
            flops=4 * ROWS * 4096, bytes_accessed=3 * MIB, transcendentals=0
        ),
        name="apply_gain",
    )(place, gain, own, rest, core_own, core_rest)


def project_kernel(place, scaled, sums, w0, w1, w2, w3, *outs):
    z, h, x = place[0], place[2], place[4]
    for part in range(2):
        columns = (x // 2) ^ part
        blocks = []
        for low, weight in enumerate(((w0, w1), (w2, w3))[part]):
            for slot in range(2):
                step = (((x & 1) ^ low) * 2 + (slot ^ h)) ^ (z & 3)
                blocks.append((weight, slot, ((step & 1) * 2) | (step // 2)))
        query = jnp.zeros((4 * ROWS, LANES), jnp.float32)
        for weight, slot, at in blocks:
            query = query + jnp.dot(
                scaled[at], weight[slot, 0:256, :], preferred_element_type=jnp.float32
            )
        q_rows = pl.ds(pl.multiple_of(columns * Q_ROWS, Q_ROWS), Q_ROWS)
        kv_rows = pl.ds(
            pl.multiple_of(KV_START + columns * KV_ROWS, KV_ROWS), KV_ROWS
        )
        for group, out in enumerate(outs):
            rows = slice(group * ROWS, (group + 1) * ROWS)
            out[q_rows, :] = query[rows].astype(jnp.bfloat16)
            total = jnp.zeros((KV_ROWS, ROWS), jnp.float32)
            for weight, slot, at in blocks:
                total = total + lax.dot_general(
                    weight[slot, 256:320, :],
                    scaled[at, rows, :],
                    (((1,), (1,)), ((), ())),
                    preferred_element_type=jnp.float32,
                )
            total = jnp.concatenate(
                [total, jnp.zeros((KV_ROWS, LANES - ROWS), jnp.float32)], axis=1
            )
            out[kv_rows, :] = total.astype(jnp.bfloat16)
    for group, out in enumerate(outs):
        out[SUM_START:PART_ROWS, :] = sums[group]


def project(place, scaled, sums, weights):
    part = jax.ShapeDtypeStruct((PART_ROWS, LANES), jnp.bfloat16)
    return pl.pallas_call(
        project_kernel,
        out_shape=(part,) * 4,
        in_specs=[smem()] + vmem(6),
        out_specs=tuple(vmem(4)),
        compiler_params=params(16),
        cost_estimate=pl.CostEstimate(
            flops=2 * ROWS * 8192 * 320, bytes_accessed=4 * MIB, transcendentals=0
        ),
        name="project",
    )(place, scaled, sums, *weights)


def reduce_kernel(place, p0, p1, p2, p3, query, sums, sent, kv):
    high = place[0] // 4

    def total(start, rows):
        if not isinstance(start, int):
            start = pl.multiple_of(start, rows)
        value = jnp.zeros((rows, LANES), jnp.float32)
        for part in (p0, p1, p2, p3):
            value = value + part[pl.ds(start, rows), :].astype(jnp.float32)
        return value

    kv[...] = total(KV_START, 2 * KV_ROWS).astype(jnp.bfloat16)
    query[...] = total(high * Q_ROWS, Q_ROWS)
    sent[0:Q_ROWS, :] = total((1 - high) * Q_ROWS, Q_ROWS).astype(jnp.bfloat16)
    squares = join_sum(total(SUM_START, SUM_ROWS))
    sums[...] = squares
    sent[Q_ROWS : Q_ROWS + SUM_ROWS, :] = split_sum(squares)


def reduce_parts(place, parts):
    return pl.pallas_call(
        reduce_kernel,
        out_shape=(
            jax.ShapeDtypeStruct((Q_ROWS, LANES), jnp.float32),
            jax.ShapeDtypeStruct((8, LANES), jnp.float32),
            jax.ShapeDtypeStruct((Q_ROWS + SUM_ROWS, LANES), jnp.bfloat16),
            jax.ShapeDtypeStruct((2 * KV_ROWS, LANES), jnp.bfloat16),
        ),
        in_specs=[smem()] + vmem(4),
        out_specs=tuple(vmem(4)),
        compiler_params=params(8),
        cost_estimate=pl.CostEstimate(
            flops=4 * MIB, bytes_accessed=2 * MIB, transcendentals=0
        ),
        name="reduce_parts",
    )(place, *parts)


def attend_kernel(
    place, lengths, query, sums, got, p0, p2, p1, p3, out, held
):
    z = place[0]
    squares = sums[...] + join_sum(got[Q_ROWS : Q_ROWS + SUM_ROWS, :])
    scale = lax.rsqrt(squares * (1.0 / 8192) + norm_eps)[0:1, :]
    for step, pair in ((0, p0), (2, p2), (1, p1), (3, p3)):
        for at in range(2):
            piece = pair[at * KV_ROWS : (at + 1) * KV_ROWS, :]
            piece = piece.astype(jnp.float32) * scale
            held[((z & 3) ^ step) * 2 + at] = piece.astype(jnp.bfloat16)
    column = jnp.broadcast_to(scale, (128, LANES)).T[0:ROWS, 0:1]
    heads = query[...] + got[0:Q_ROWS, :].astype(jnp.float32)
    heads = (heads * column).astype(jnp.bfloat16)
    query_at = lax.broadcasted_iota(jnp.int32, (ROWS, LANES), 0)
    key_at = lax.broadcasted_iota(jnp.int32, (ROWS, LANES), 1)
    query_doc = jnp.zeros((ROWS, LANES), jnp.int32)
    key_doc = jnp.zeros((ROWS, LANES), jnp.int32)
    end = 0
    for doc in range(4):
        end = end + lengths[0, doc]
        query_doc = query_doc + (query_at >= end).astype(jnp.int32)
        key_doc = key_doc + (key_at >= end).astype(jnp.int32)
    allowed = (query_doc == key_doc) & (key_at <= query_at)
    for head in range(2):
        keys = held[head * 4 : head * 4 + 4, 0:32, :].reshape(HEAD_DIM, LANES)
        values = held[head * 4 : head * 4 + 4, 32:64, :].reshape(HEAD_DIM, LANES)
        columns = slice(head * HEAD_DIM, (head + 1) * HEAD_DIM)
        scores = jnp.dot(heads[:, columns], keys, preferred_element_type=jnp.float32)
        scores = jnp.where(allowed, scores * HEAD_DIM**-0.5, -1e30)
        scores = scores - jnp.max(scores, axis=-1, keepdims=True)
        weights = jnp.exp(scores)
        weights = weights / jnp.sum(weights, axis=-1, keepdims=True)
        context = lax.dot_general(
            weights.astype(jnp.bfloat16),
            values,
            (((1,), (1,)), ((), ())),
            preferred_element_type=jnp.float32,
        )
        out[:, columns] = context.astype(jnp.bfloat16)


def attend(place, lengths, query, sums, got, pairs):
    return pl.pallas_call(
        attend_kernel,
        out_shape=jax.ShapeDtypeStruct((ROWS, 256), jnp.bfloat16),
        in_specs=[smem(), smem()] + vmem(7),
        out_specs=vmem(1)[0],
        scratch_shapes=[pltpu.VMEM((8, KV_ROWS, LANES), jnp.bfloat16)],
        compiler_params=params(8),
        cost_estimate=pl.CostEstimate(
            flops=8 * ROWS * ROWS * HEAD_DIM,
            bytes_accessed=MIB // 2,
            transcendentals=2 * ROWS * ROWS,
        ),
        name="attend",
    )(place, lengths, query, sums, got, *pairs)


def output_kernel(place, p0, p2, p1, p3, weight, out, *, other):
    start = pl.multiple_of((place[1] ^ other) * 512, 512)
    total = jnp.zeros((ROWS, 512), jnp.float32)
    for at in range(8):
        part = (p0, p2, p1, p3)[at // 2][at % 2]
        total = total + jnp.dot(
            part,
            weight[place[0] ^ ORDER[at], :, pl.ds(start, 512)],
            preferred_element_type=jnp.float32,
        )
    out[...] = total.astype(out.dtype)


def project_output(place, pairs, weight, other):
    def kernel(*refs):
        output_kernel(*refs, other=other)

    return pl.pallas_call(
        kernel,
        out_shape=jax.ShapeDtypeStruct(
            (ROWS, 512), jnp.bfloat16 if other else jnp.float32
        ),
        in_specs=[smem()] + vmem(5),
        out_specs=vmem(1)[0],
        compiler_params=params(24),
        cost_estimate=pl.CostEstimate(
            flops=2 * ROWS * 2048 * 512, bytes_accessed=5 * MIB, transcendentals=0
        ),
        name="output_other" if other else "output_own",
    )(place, *pairs, weight)


def shards(
    tokens,
    norm_gain,
    doc_lengths,
    query_master,
    query_grad,
    query_first,
    query_second,
    kv_master,
    kv_grad,
    kv_first,
    kv_second,
    out_master,
    out_grad,
    out_first,
    out_second,
):
    place = [lax.axis_index(name) for name in ("z", "c", "h", "y", "x")]
    y = place[3]
    place = jnp.stack(place).astype(jnp.int32)

    with jax.named_scope("adam"):
        q_master, q_first, q_second, q_weight = adam_step(
            query_master, query_grad, query_first, query_second
        )
        k_master, k_first, k_second, k_weight = adam_step(
            kv_master, kv_grad, kv_first, kv_second
        )
        o_master, o_first, o_second, o_weight = adam_step(
            out_master, out_grad, out_first, out_second
        )

    with jax.named_scope("in_weight"):
        k_rows = k_weight.transpose(0, 2, 1).reshape(KV_ROWS, 256)
        weights = [
            jnp.concatenate([move_weight(q_weight, flip, 0), move_weight(k_rows, flip, 1)])
            for flip in range(2)
        ]
        weights = jnp.stack(weights)

    with jax.named_scope("tokens"):
        own = spread_groups(tokens, y)
        core_own = swap_core(own)
        moved = after(own, weights)
        rest = jnp.stack([swap_z(moved, step) for step in BLOCK[1:]])
        weights = [weights] + [swap_line(weights, "x", bits) for bits in (1, 2, 3)]
        core_rest = swap_core(after(rest, *weights))
        gain = norm_gain.reshape(32, 1, LANES)
        scaled, sums = apply_gain(
            place, gain, own, rest, core_own, core_rest
        )

    with jax.named_scope("projections"):
        parts = project(place, scaled, sums, weights)
        parts = [parts[0]] + [swap_line(parts[n], "y", n) for n in (1, 2, 3)]
        query, sums, sent, kv = reduce_parts(place, parts)
        kv = kv.astype(jnp.float32) + swap_z(kv, 4).astype(jnp.float32)
        kv = kv.astype(jnp.bfloat16)
        got = swap_z(after(sent, kv), 4)
        pieces = gather_line(kv)

    with jax.named_scope("out_columns"):
        o_rows = lax.all_gather(after(o_weight, weights[0]), ("h", "z"), axis=0, tiled=False)
        start = lax.axis_index("z") * 1024
        o_rows = after(o_rows, query)
        o_halves = lax.dynamic_slice_in_dim(o_rows, start, 1024, axis=2)
        o_halves = o_halves.reshape(2, 8, 8, 1024)

    with jax.named_scope("out_weight"):
        o_whole = lax.all_gather(o_halves, ("x", "y"), axis=0, tiled=False)
        o_whole = o_whole.reshape(4, 4, 2, 8, 8, 1024).transpose(3, 0, 2, 1, 4, 5)
        o_whole = o_whole.reshape(8, 256, 1024)

    with jax.named_scope("attention"):
        context = attend(place, doc_lengths, query, sums, got, pieces)
        context = gather_line(jnp.stack([context, swap_z(context, 4)]))

    with jax.named_scope("output"):
        sent = swap_core(project_output(place, context, o_whole, 1))
        kept = project_output(place, context, o_whole, 0)
        mixed = (kept + sent.astype(jnp.float32)).astype(jnp.bfloat16)

    return (
        mixed,
        q_master,
        q_first,
        q_second,
        k_master,
        k_first,
        k_second,
        o_master,
        o_first,
        o_second,
    )


def solution(mesh):
    pool, tp = ("x", "h", "y"), ("z", "c")
    split = Mesh(mesh.devices.reshape(4, 2, 4, 8, 2), ("x", "h", "y", "z", "c"))
    weight = P(pool, tp)
    kv_weight = P(None, pool, tp)
    out_weight = P(tp + pool, None)
    in_specs = (
        (P(pool, tp), P(), P(pool, None))
        + (weight,) * 4
        + (kv_weight,) * 4
        + (out_weight,) * 4
    )
    out_specs = (P(pool, tp),) + (weight,) * 3 + (kv_weight,) * 3 + (out_weight,) * 3
    return jax.shard_map(
        shards, mesh=split, in_specs=in_specs, out_specs=out_specs, check_vma=False
    )
```

```python
import jax
import jax.numpy as jnp
from jax import lax
from jax.experimental import pallas as pl
from jax.experimental.pallas import tpu as pltpu
from jax.sharding import Mesh, PartitionSpec as P

HEAD_DIM = 128
ROWS = 192
LANES = 256
MIB = 1 << 20

beta_first = 0.9
beta_second = 0.95
learn_rate = 0.001
adam_eps = 1e-08
norm_eps = 1e-06

ORDER = (0, 4, 2, 6, 1, 5, 3, 7)
BLOCK = (0, 2, 1, 3)

Q_ROWS, KV_ROWS, SUM_ROWS = 192, 64, 16
KV_START, SUM_START = 2 * Q_ROWS, 2 * Q_ROWS + 2 * KV_ROWS
PART_ROWS = SUM_START + SUM_ROWS


def adam_step(master, gradient, first, second):
    grad_value = gradient.astype(jnp.float32)
    first = beta_first * first + (1.0 - beta_first) * grad_value
    second = beta_second * second + (1.0 - beta_second) * grad_value * grad_value
    correct_first = 1.0 - beta_first**10
    correct_second = 1.0 - beta_second**10
    master = master - learn_rate * (first / correct_first) / (
        jnp.sqrt(second / correct_second) + adam_eps
    )
    return (master, first, second, master.astype(jnp.bfloat16))


def swap_z(value, bit):
    return lax.ppermute(value, "z", [(z, z ^ bit) for z in range(8)])


def swap_core(value):
    return lax.ppermute(value, "c", [(0, 1), (1, 0)])


def gather_line(pair):
    return [pair] + [swap_z(pair, step) for step in (2, 1, 3)]


def swap_line(value, axis, bits):
    return lax.ppermute(value, axis, [(at, at ^ bits) for at in range(4)])


def move_weight(value, flip, turn_core):
    moves = []
    for x in range(4):
        for h in range(2):
            for y in range(4):
                for z in range(8):
                    for c in range(2):
                        to_x, to_c = (c, z // 4) if turn_core else (z // 4, c)
                        to_x, to_z = to_x * 2 + x % 2, (x // 2) * 4 + z % 4
                        source = (((x * 2 + h) * 4 + y) * 8 + z) * 2 + c
                        target = (((to_x * 2 + (h ^ flip)) * 4 + y) * 8 + to_z) * 2
                        moves.append((source, target + to_c))
    return lax.ppermute(value, ("x", "h", "y", "z", "c"), moves)


def spread_groups(tokens, y):
    halves = tokens.reshape(ROWS, 2, LANES).transpose(1, 0, 2)
    got = []
    for turn in range(2):
        moves = []
        for at in range(4):
            for c in range(2):
                block = (at % 2) ^ turn
                moves.append((at * 2 + c, (c * 2 + block) * 2 + at // 2))
        piece = jnp.where(y % 2 == 0, halves[turn], halves[1 - turn])
        got.append(lax.ppermute(piece, ("y", "c"), moves))
    return jnp.stack(got)


def after(value, *others):
    return lax.optimization_barrier((value,) + others)[0]


def vmem(count):
    return [pl.BlockSpec(memory_space=pltpu.VMEM)] * count


def smem():
    return pl.BlockSpec(memory_space=pltpu.SMEM)


def params(mib):
    return pltpu.CompilerParams(vmem_limit_bytes=mib * MIB)


def lanes_of(column):
    wide = jnp.broadcast_to(column, (ROWS, 128))
    wide = jnp.concatenate([wide, jnp.zeros((LANES - ROWS, 128), jnp.float32)])
    return wide.T[0:8]


def split_sum(rows):
    high = rows.astype(jnp.bfloat16)
    low = (rows - high.astype(jnp.float32)).astype(jnp.bfloat16)
    return jnp.concatenate([high, low])


def join_sum(rows):
    rows = rows.astype(jnp.float32)
    return rows[0:8] + rows[8:16]


def gain_kernel(place, gain, own, rest, core_own, core_rest, out, sums):
    z, c, y = place[0], place[1], place[3]
    for other, (first, others) in enumerate(((own, rest), (core_own, core_rest))):
        for turn in range(2):
            group = ((c ^ other) ^ (y // 2)) * 2 + turn
            rows = pl.ds(pl.multiple_of(group * ROWS, ROWS), ROWS)
            total = jnp.zeros((ROWS, LANES), jnp.float32)
            for at in range(4):
                value = first[turn] if at == 0 else others[at - 1, turn]
                value = value.astype(jnp.float32)
                total = total + value * value
                value = value * gain[(z ^ BLOCK[at]) * 4 + y]
                out[at, rows, :] = value.astype(jnp.bfloat16)
            column = jnp.sum(total, axis=-1, keepdims=True)
            sums[group] = split_sum(lanes_of(column))


def apply_gain(place, gain, own, rest, core_own, core_rest):
    return pl.pallas_call(
        gain_kernel,
        out_shape=(
            jax.ShapeDtypeStruct((4, 4 * ROWS, LANES), jnp.bfloat16),
            jax.ShapeDtypeStruct((4, SUM_ROWS, LANES), jnp.bfloat16),
        ),
        in_specs=[smem()] + vmem(5),
        out_specs=tuple(vmem(2)),
        compiler_params=params(12),
        cost_estimate=pl.CostEstimate(
            flops=4 * ROWS * 4096, bytes_accessed=3 * MIB, transcendentals=0
        ),
        name="apply_gain",
    )(place, gain, own, rest, core_own, core_rest)


def project_kernel(place, scaled, sums, w0, w1, w2, w3, *outs):
    z, h, x = place[0], place[2], place[4]
    for part in range(2):
        columns = (x // 2) ^ part
        blocks = []
        for low, weight in enumerate(((w0, w1), (w2, w3))[part]):
            for slot in range(2):
                step = (((x & 1) ^ low) * 2 + (slot ^ h)) ^ (z & 3)
                blocks.append((weight, slot, ((step & 1) * 2) | (step // 2)))
        query = jnp.zeros((4 * ROWS, LANES), jnp.float32)
        for weight, slot, at in blocks:
            query = query + jnp.dot(
                scaled[at], weight[slot, 0:256, :], preferred_element_type=jnp.float32
            )
        q_rows = pl.ds(pl.multiple_of(columns * Q_ROWS, Q_ROWS), Q_ROWS)
        kv_rows = pl.ds(
            pl.multiple_of(KV_START + columns * KV_ROWS, KV_ROWS), KV_ROWS
        )
        for group, out in enumerate(outs):
            rows = slice(group * ROWS, (group + 1) * ROWS)
            out[q_rows, :] = query[rows].astype(jnp.bfloat16)
            total = jnp.zeros((KV_ROWS, ROWS), jnp.float32)
            for weight, slot, at in blocks:
                total = total + lax.dot_general(
                    weight[slot, 256:320, :],
                    scaled[at, rows, :],
                    (((1,), (1,)), ((), ())),
                    preferred_element_type=jnp.float32,
                )
            total = jnp.concatenate(
                [total, jnp.zeros((KV_ROWS, LANES - ROWS), jnp.float32)], axis=1
            )
            out[kv_rows, :] = total.astype(jnp.bfloat16)
    for group, out in enumerate(outs):
        out[SUM_START:PART_ROWS, :] = sums[group]


def project(place, scaled, sums, weights):
    part = jax.ShapeDtypeStruct((PART_ROWS, LANES), jnp.bfloat16)
    return pl.pallas_call(
        project_kernel,
        out_shape=(part,) * 4,
        in_specs=[smem()] + vmem(6),
        out_specs=tuple(vmem(4)),
        compiler_params=params(16),
        cost_estimate=pl.CostEstimate(
            flops=2 * ROWS * 8192 * 320, bytes_accessed=4 * MIB, transcendentals=0
        ),
        name="project",
    )(place, scaled, sums, *weights)


def reduce_kernel(place, p0, p1, p2, p3, query, sums, sent, kv):
    high = place[0] // 4

    def total(start, rows):
        if not isinstance(start, int):
            start = pl.multiple_of(start, rows)
        value = jnp.zeros((rows, LANES), jnp.float32)
        for part in (p0, p1, p2, p3):
            value = value + part[pl.ds(start, rows), :].astype(jnp.float32)
        return value

    kv[...] = total(KV_START, 2 * KV_ROWS).astype(jnp.bfloat16)
    query[...] = total(high * Q_ROWS, Q_ROWS)
    sent[0:Q_ROWS, :] = total((1 - high) * Q_ROWS, Q_ROWS).astype(jnp.bfloat16)
    squares = join_sum(total(SUM_START, SUM_ROWS))
    sums[...] = squares
    sent[Q_ROWS : Q_ROWS + SUM_ROWS, :] = split_sum(squares)


def reduce_parts(place, parts):
    return pl.pallas_call(
        reduce_kernel,
        out_shape=(
            jax.ShapeDtypeStruct((Q_ROWS, LANES), jnp.float32),
            jax.ShapeDtypeStruct((8, LANES), jnp.float32),
            jax.ShapeDtypeStruct((Q_ROWS + SUM_ROWS, LANES), jnp.bfloat16),
            jax.ShapeDtypeStruct((2 * KV_ROWS, LANES), jnp.bfloat16),
        ),
        in_specs=[smem()] + vmem(4),
        out_specs=tuple(vmem(4)),
        compiler_params=params(8),
        cost_estimate=pl.CostEstimate(
            flops=4 * MIB, bytes_accessed=2 * MIB, transcendentals=0
        ),
        name="reduce_parts",
    )(place, *parts)


def attend_kernel(
    place, lengths, query, sums, got, p0, p2, p1, p3, out, held, held_values
):
    z = place[0]
    squares = sums[...] + join_sum(got[Q_ROWS : Q_ROWS + SUM_ROWS, :])
    scale = lax.rsqrt(squares * (1.0 / 8192) + norm_eps)[0:1, :]
    for step, pair in ((0, p0), (2, p2), (1, p1), (3, p3)):
        chip = (z & 3) ^ step
        parts = []
        for at in range(2):
            part = pair[at * KV_ROWS : (at + 1) * KV_ROWS, :]
            part = part.astype(jnp.float32) * scale
            held[chip * 2 + at] = part[0:32].astype(jnp.bfloat16)
            parts.append(part[32:64])
        rows = [part[n : n + 8] for n in range(0, 32, 8) for part in parts]
        held_values[chip] = jnp.concatenate(rows).astype(jnp.bfloat16)
    column = jnp.broadcast_to(scale, (128, LANES)).T[0:ROWS, 0:1]
    heads = query[...] + got[0:Q_ROWS, :].astype(jnp.float32)
    heads = (heads * column).astype(jnp.bfloat16)
    query_at = lax.broadcasted_iota(jnp.int32, (ROWS, LANES), 0)
    key_at = lax.broadcasted_iota(jnp.int32, (ROWS, LANES), 1)
    query_doc = jnp.zeros((ROWS, LANES), jnp.int32)
    key_doc = jnp.zeros((ROWS, LANES), jnp.int32)
    end = 0
    for doc in range(4):
        end = end + lengths[0, doc]
        query_doc = query_doc + (query_at >= end).astype(jnp.int32)
        key_doc = key_doc + (key_at >= end).astype(jnp.int32)
    allowed = (query_doc == key_doc) & (key_at <= query_at)
    for head in range(2):
        keys = held[head * 4 : head * 4 + 4].reshape(HEAD_DIM, LANES)
        values = held_values[head * 2 : head * 2 + 2].reshape(HEAD_DIM, LANES)
        columns = slice(head * HEAD_DIM, (head + 1) * HEAD_DIM)
        scores = jnp.dot(heads[:, columns], keys, preferred_element_type=jnp.float32)
        scores = jnp.where(allowed, scores * HEAD_DIM**-0.5, -1e30)
        scores = scores - jnp.max(scores, axis=-1, keepdims=True)
        weights = jnp.exp(scores)
        weights = weights / jnp.sum(weights, axis=-1, keepdims=True)
        context = lax.dot_general(
            weights.astype(jnp.bfloat16),
            values,
            (((1,), (1,)), ((), ())),
            preferred_element_type=jnp.float32,
        )
        out[:, columns] = context.astype(jnp.bfloat16)


def attend(place, lengths, query, sums, got, pairs):
    return pl.pallas_call(
        attend_kernel,
        out_shape=jax.ShapeDtypeStruct((ROWS, 256), jnp.bfloat16),
        in_specs=[smem(), smem()] + vmem(7),
        out_specs=vmem(1)[0],
        scratch_shapes=[
            pltpu.VMEM((8, 32, LANES), jnp.bfloat16),
            pltpu.VMEM((4, 64, LANES), jnp.bfloat16),
        ],
        compiler_params=params(8),
        cost_estimate=pl.CostEstimate(
            flops=8 * ROWS * ROWS * HEAD_DIM,
            bytes_accessed=MIB // 2,
            transcendentals=2 * ROWS * ROWS,
        ),
        name="attend",
    )(place, lengths, query, sums, got, *pairs)


def output_kernel(place, p0, p2, p1, p3, weight, out, *, other):
    start = pl.multiple_of((place[1] ^ other) * 512, 512)
    total = jnp.zeros((ROWS, 512), jnp.float32)
    for at in range(8):
        part = (p0, p2, p1, p3)[at // 2][at % 2]
        total = total + jnp.dot(
            part,
            weight[:, place[0] ^ ORDER[at], :, pl.ds(start, 512)].reshape(256, 512),
            preferred_element_type=jnp.float32,
        )
    out[...] = total.astype(out.dtype)


def project_output(place, pairs, weight, other):
    def kernel(*refs):
        output_kernel(*refs, other=other)

    return pl.pallas_call(
        kernel,
        out_shape=jax.ShapeDtypeStruct(
            (ROWS, 512), jnp.bfloat16 if other else jnp.float32
        ),
        in_specs=[smem()] + vmem(5),
        out_specs=vmem(1)[0],
        compiler_params=params(56),
        cost_estimate=pl.CostEstimate(
            flops=2 * ROWS * 2048 * 512, bytes_accessed=5 * MIB, transcendentals=0
        ),
        name="output_other" if other else "output_own",
    )(place, *pairs, weight)


def shards(
    tokens,
    norm_gain,
    doc_lengths,
    query_master,
    query_grad,
    query_first,
    query_second,
    kv_master,
    kv_grad,
    kv_first,
    kv_second,
    out_master,
    out_grad,
    out_first,
    out_second,
):
    place = [lax.axis_index(name) for name in ("z", "c", "h", "y", "x")]
    y = place[3]
    place = jnp.stack(place).astype(jnp.int32)

    with jax.named_scope("adam"):
        q_master, q_first, q_second, q_weight = adam_step(
            query_master, query_grad, query_first, query_second
        )
        k_master, k_first, k_second, k_weight = adam_step(
            kv_master, kv_grad, kv_first, kv_second
        )
        o_master, o_first, o_second, o_weight = adam_step(
            out_master, out_grad, out_first, out_second
        )

    with jax.named_scope("in_weight"):
        k_rows = k_weight.transpose(0, 2, 1).reshape(KV_ROWS, 256)
        weights = [
            jnp.concatenate([move_weight(q_weight, flip, 0), move_weight(k_rows, flip, 1)])
            for flip in range(2)
        ]
        weights = jnp.stack(weights)

    with jax.named_scope("tokens"):
        own = spread_groups(tokens, y)
        core_own = swap_core(own)
        moved = after(own, weights)
        rest = jnp.stack([swap_z(moved, step) for step in BLOCK[1:]])
        weights = [weights] + [swap_line(weights, "x", bits) for bits in (1, 2, 3)]
        core_rest = swap_core(after(rest, *weights))
        gain = norm_gain.reshape(32, 1, LANES)
        scaled, sums = apply_gain(
            place, gain, own, rest, core_own, core_rest
        )

    with jax.named_scope("projections"):
        parts = project(place, scaled, sums, weights)
        parts = [parts[0]] + [swap_line(parts[n], "y", n) for n in (1, 2, 3)]
        query, sums, sent, kv = reduce_parts(place, parts)
        kv = kv.astype(jnp.float32) + swap_z(kv, 4).astype(jnp.float32)
        kv = kv.astype(jnp.bfloat16)
        got = swap_z(after(sent, kv), 4)
        pieces = gather_line(kv)

    with jax.named_scope("out_columns"):
        o_rows = lax.all_gather(after(o_weight, weights[0]), ("h", "z"), axis=0, tiled=False)
        start = lax.axis_index("z") * 1024
        o_rows = after(o_rows, query)
        o_halves = lax.dynamic_slice_in_dim(o_rows, start, 1024, axis=2)
        o_halves = o_halves.reshape(2, 8, 8, 1024).transpose(1, 0, 2, 3)
        o_halves = o_halves.reshape(8, 16, 1024)

    with jax.named_scope("out_weight"):
        o_whole = lax.all_gather(o_halves, ("x", "y"), axis=0, tiled=False)

    with jax.named_scope("attention"):
        context = attend(place, doc_lengths, query, sums, got, pieces)
        context = gather_line(jnp.stack([context, swap_z(context, 4)]))

    with jax.named_scope("output"):
        sent = swap_core(project_output(place, context, o_whole, 1))
        kept = project_output(place, context, o_whole, 0)
        mixed = (kept + sent.astype(jnp.float32)).astype(jnp.bfloat16)

    return (
        mixed,
        q_master,
        q_first,
        q_second,
        k_master,
        k_first,
        k_second,
        o_master,
        o_first,
        o_second,
    )


def solution(mesh):
    pool, tp = ("x", "h", "y"), ("z", "c")
    split = Mesh(mesh.devices.reshape(4, 2, 4, 8, 2), ("x", "h", "y", "z", "c"))
    weight = P(pool, tp)
    kv_weight = P(None, pool, tp)
    out_weight = P(tp + pool, None)
    in_specs = (
        (P(pool, tp), P(), P(pool, None))
        + (weight,) * 4
        + (kv_weight,) * 4
        + (out_weight,) * 4
    )
    out_specs = (P(pool, tp),) + (weight,) * 3 + (kv_weight,) * 3 + (out_weight,) * 3
    return jax.shard_map(
        shards, mesh=split, in_specs=in_specs, out_specs=out_specs, check_vma=False
    )
```
